32 devices in a mesh: sub: 4 (over y, core), grp: 8 (over z, x).
Axes of the slice: x: 2, y: 2, z: 4, core: 2. Of those that a mesh axis runs over, the one named last changes fastest.
Arguments:
- schur: bfloat16 [64, 1024, 1024], P(('sub', 'grp')), may hold values from -1 to 17, as said below
- local_inverse: bfloat16 [64, 1024, 1024], P(('sub', 'grp')), may hold values from -1 to 2, as said below
- coupling: float32 [64, 256], P(('sub', 'grp')), may hold values from 0.5 to 1.5
- basis: bfloat16 [64, 24, 1024], P(('sub', 'grp')), may hold values from -0.1875 to 0.1875
- coarse_map: int32 [64, 24], P(('sub', 'grp')), may hold values from 0 to 511
- coarse_count: int32 [64], P(('sub', 'grp')), may hold values from 12 to 24, as said below
- diag_inverse: float32 [16, 256, 256], P('grp'), may hold values from -1 to 1
- chain_factor: float32 [16, 256, 256], P('grp'), may hold values from -2 to 1
- residual: float32 [64, 1024, 384], P(('sub', 'grp')), may hold values from -18 to 18
- direction: float32 [64, 1024, 384], P(('sub', 'grp')), may hold values from -6 to 6
- rz_prev: float32 [384], replicated, may hold values from 32768 to 327680
Outputs:
- update: float32 [64, 1024, 384], P(('sub', 'grp'))
- residual_new: float32 [64, 1024, 384], P(('sub', 'grp'))
The draws below stay inside these ranges and needn't reach their ends.
Inputs may be any that keep to these rules, and one draw needn't show every extreme that they name: `schur`: each block is symmetric positive definite. `local_inverse`: each block is symmetric positive definite. `coarse_count`: the first subdomain of each device has exactly 24 live slots.
All inputs are finite; a program needn't handle non-finite values.
Results may differ from the reference program's by a relative error of at most 0.0033.
Values sent between devices are 32-bit elements; how exact they have to be, the bound alone decides.
A program may use at most 64 MiB of HBM per device.

```python
import math
import jax
import jax.numpy as jnp
from jax import lax

F = 1024
SHARE = 256
CMAX = 24
BLK = 256
NRHS = 384
SUBS_DEV = 2
NSUB = 64
NCG = 512
NSN = 16
N_GRP = 8


def kernel_blocks(key, block_count, order_size, scale_factor):
    positions = jnp.arange(order_size, dtype=jnp.float32)
    kernel = 0.25 * jnp.exp(-jnp.abs(positions[:, None] - positions[None, :]) / (order_size / 32.0))
    identity = jnp.eye(order_size, dtype=jnp.float32)

    def one_block(block_index):
        block_key = jax.random.fold_in(key, block_index)
        noise_key, scale_key = jax.random.split(block_key)
        noise_part = jax.random.uniform(noise_key, (order_size, order_size), jnp.float32, -1.0, 1.0) / order_size
        noise_part = 0.5 * (noise_part + noise_part.T)
        row_scale = jnp.exp(jax.random.uniform(scale_key, (order_size,), jnp.float32, jnp.log(0.7), jnp.log(1.4)))
        core_part = kernel + noise_part + 8.0 * identity
        return (scale_factor * row_scale[:, None] * core_part * row_scale[None, :]).astype(jnp.bfloat16)
    return lax.map(one_block, jnp.arange(block_count, dtype=jnp.int32))


def draw_schur(key, part):
    key = jax.random.fold_in(key, 3)
    return kernel_blocks(key, NSUB, F, 1.0)


def draw_local_inverse(key, part):
    key = jax.random.fold_in(key, 5)
    return kernel_blocks(key, NSUB, F, 0.0625)


def draw_coarse_count(key, part):
    key = jax.random.fold_in(key, 7)
    counts = jax.random.randint(key, (NSUB,), CMAX // 2, CMAX + 1, jnp.int32)
    first_slot = jnp.arange(NSUB, dtype=jnp.int32) % SUBS_DEV == 0
    return jnp.where(first_slot, CMAX, counts).astype(jnp.int32)


def draw_diag_inverse(key, part):
    key = jax.random.fold_in(key, 11)
    diag_key, noise_key = jax.random.split(key)
    diagonal = jnp.exp(jax.random.uniform(diag_key, (NSN, BLK), jnp.float32, jnp.log(0.1), jnp.log(0.4)))
    noise_part = jnp.clip(jax.random.normal(noise_key, (NSN, BLK, BLK), jnp.float32), -4.0, 4.0) * (0.1 / BLK ** 0.5)
    identity = jnp.eye(BLK, dtype=jnp.float32)
    return noise_part + diagonal[:, :, None] * identity[None]


def draw_chain_factor(key, part):
    key = jax.random.fold_in(key, 13)
    flag_key, fast_key, noise_key = jax.random.split(key, 3)
    fast_rate = jnp.exp(jax.random.uniform(fast_key, (NSN, BLK), jnp.float32, jnp.log(0.3), jnp.log(0.6)))
    slow_flag = jax.random.uniform(flag_key, (BLK,), jnp.float32) < 0.5
    slow_rate = jnp.exp(jnp.log(0.25) / NSN)
    rate = jnp.where(slow_flag[None, :], slow_rate, fast_rate)
    noise_part = jnp.clip(jax.random.normal(noise_key, (NSN, BLK, BLK), jnp.float32), -4.0, 4.0) * (0.15 / BLK ** 0.5)
    identity = jnp.eye(BLK, dtype=jnp.float32)
    return noise_part - rate[:, :, None] * identity[None]


def draw_residual(key, part):
    key = jax.random.fold_in(key, 17)
    base_key = jax.random.fold_in(key, 0)
    rise = 3.0 ** (jnp.arange(NSUB, dtype=jnp.float32) / (NSUB - 1))
    values = jnp.clip(jax.random.normal(base_key, (NSUB, F, NRHS), jnp.float32), -6.0, 6.0)
    return values * rise[:, None, None]


def plant(entries, rng, smallest, top_value):
    extent = entries.shape
    spot = [jax.random.randint(jax.random.fold_in(rng, axis), (), 0, extent[axis]) for axis in range(len(extent))]
    entries = entries.at[tuple(spot)].set(smallest)
    longest = extent.index(max(extent))
    spot[longest] = (spot[longest] + 1) % extent[longest]
    return entries.at[tuple(spot)].set(top_value)


def block_levels(rng, extent, cuts, smallest, largest):
    factor_of, own = 1.0, jax.random.fold_in(rng, 6)
    for position, parts in cuts:
        draws = jnp.exp(jax.random.uniform(jax.random.fold_in(own, position), (parts,), jnp.float32, smallest / len(cuts), largest / len(cuts)))
        factor_of = factor_of * jnp.repeat(draws, extent[position] // parts).reshape([-1 if axis == position else 1 for axis in range(len(extent))])
    return factor_of


def centred(stream_key, dims, scale, limit, cuts=(), held_as=jnp.bfloat16):
    entries = jax.random.normal(stream_key, dims, jnp.float32) * scale
    if len(cuts) > 0:
        entries = block_levels(stream_key, dims, cuts, -0.22, 0.18) * entries
    return jnp.clip(entries, min=-limit, max=limit).astype(held_as)


def setup_inputs(seed: int = 0) -> dict:
    streams_of = jax.random.split(jax.random.key(seed), 12)
    schur = draw_schur(jax.random.fold_in(streams_of[11], 71), 0)
    local_inverse = draw_local_inverse(jax.random.fold_in(streams_of[11], 71), 0)
    coupling = jnp.clip(0.5 + 1.0 * jax.random.uniform(streams_of[2], (NSUB, SHARE), jnp.float32) ** block_levels(streams_of[2], (NSUB, SHARE), ((0, 32),), -0.2, 0.2), 0.5, 1.5)
    basis = centred(streams_of[3], (NSUB, CMAX, F), F ** -0.5, 0.1875, ((0, 32),))
    coarse_map = plant(jax.random.randint(streams_of[4], (NSUB, CMAX), 0, NCG), jax.random.fold_in(streams_of[4], 1), 0, NCG - 1).astype(jnp.int32)
    coarse_count = draw_coarse_count(jax.random.fold_in(streams_of[11], 71), 0)
    diag_inverse = draw_diag_inverse(jax.random.fold_in(streams_of[11], 71), 0)
    chain_factor = draw_chain_factor(jax.random.fold_in(streams_of[11], 71), 0)
    residual = draw_residual(jax.random.fold_in(streams_of[11], 71), 0)
    direction = centred(streams_of[9], (NSUB, F, NRHS), 1.0, 6.0, ((0, 32),), jnp.float32)
    rz_prev = jnp.clip(jnp.exp(jax.random.uniform(streams_of[10], (NRHS,), jnp.float32, math.log(32768.0), math.log(327680.0))), 32768.0, 327680.0)
    return dict(schur=schur, local_inverse=local_inverse, coupling=coupling, basis=basis, coarse_map=coarse_map, coarse_count=coarse_count, diag_inverse=diag_inverse, chain_factor=chain_factor, residual=residual, direction=direction, rz_prev=rz_prev)


def product(left_side, right_side):
    return jnp.dot(left_side, right_side, precision=lax.Precision.HIGHEST, preferred_element_type=jnp.float32)


def forward_chain(sources, incoming, inverses, factors):
    def advance(carried, pieces):
        inverse_block, factor_block, source_block = pieces
        fresh_value = product(inverse_block, source_block) - product(factor_block, carried)
        return fresh_value, fresh_value
    last_value, values = lax.scan(advance, incoming, (inverses, factors, sources))
    return values, last_value


def backward_chain(values, incoming, inverses, factors):
    def advance(carried, pieces):
        inverse_block, factor_block, value_block = pieces
        held_value = value_block - carried
        return product(factor_block.T, held_value), product(inverse_block.T, held_value)
    outgoing, solved = lax.scan(advance, incoming, (inverses, factors, values), reverse=True)
    return outgoing, solved


def block_apply(matrices, vectors):
    def single(pieces):
        return jnp.dot(pieces[0], pieces[1], preferred_element_type=jnp.float32)
    return lax.map(single, (matrices, vectors))


def reference(schur, local_inverse, coupling, basis, coarse_map, coarse_count, diag_inverse, chain_factor, residual, direction, rz_prev):
    residual_low = residual.astype(jnp.bfloat16)
    local_part = block_apply(local_inverse, residual_low)
    basis_wide = basis.astype(jnp.float32)
    coarse_local = jnp.einsum("scf,sfn->scn", basis_wide, residual, precision=lax.Precision.HIGHEST)
    slot_index = jnp.arange(CMAX, dtype=jnp.int32)
    live_slots = (slot_index[None, :] < coarse_count[:, None]).astype(jnp.float32)
    group_index = (jnp.arange(NSUB, dtype=jnp.int32) // SUBS_DEV) % N_GRP
    global_rows = (group_index[:, None] * NCG + coarse_map).astype(jnp.int32)
    masked = coarse_local * live_slots[:, :, None]
    coarse_rhs = jax.ops.segment_sum(masked.reshape(NSUB * CMAX, NRHS), global_rows.reshape(NSUB * CMAX), num_segments=NSN * BLK)
    zero_in = jnp.zeros((BLK, NRHS), jnp.float32)
    values, last_value = forward_chain(coarse_rhs.reshape(NSN, BLK, NRHS), zero_in, diag_inverse, chain_factor)
    outgoing, solved = backward_chain(values, zero_in, diag_inverse, chain_factor)
    coarse_sol = solved.reshape(NSN * BLK, NRHS)
    correction = coarse_sol[global_rows] * live_slots[:, :, None]
    precond = local_part + jnp.einsum("scf,scn->sfn", basis_wide, correction, precision=lax.Precision.HIGHEST)
    precond_dot = jnp.sum(residual * precond, axis=(0, 1))
    new_dir = precond + (precond_dot / rz_prev) * direction
    dir_low = new_dir.astype(jnp.bfloat16)
    applied = block_apply(schur, dir_low)
    empty_face = jnp.zeros((1, SHARE, NRHS), jnp.float32)
    prev_upper = jnp.concatenate([empty_face, new_dir[:-1, F - SHARE:]], 0)
    lower_term = coupling[:, :, None] * prev_upper
    sent_back = coupling[:, :, None] * new_dir[:, :SHARE]
    upper_term = jnp.concatenate([sent_back[1:], empty_face], 0)
    middle = jnp.zeros((NSUB, F - 2 * SHARE, NRHS), jnp.float32)
    applied = applied - jnp.concatenate([lower_term, middle, upper_term], 1)
    curve_dot = jnp.sum(new_dir * applied, axis=(0, 1))
    step_size = precond_dot / curve_dot
    return step_size * new_dir, residual - step_size * applied
```

```python
import functools

import jax
import jax.numpy as jnp
from jax import lax
from jax.experimental import pallas as pl
from jax.experimental.pallas import tpu as pltpu
from jax.sharding import PartitionSpec as P

F32 = jnp.float32
BF16 = jnp.bfloat16
NN = (((1,), (0,)), ((), ()))
NT = (((1,), (1,)), ((), ()))
LANE = 128
CHUNK = 256


def mm(a, b, dims=NN):
    return lax.dot_general(a, b, dims, preferred_element_type=F32)


def split(x):
    hi = x.astype(BF16)
    return hi, (x - hi.astype(F32)).astype(BF16)


def mm3(a, b, dims=NN):
    return mm(a[0], b[0], dims) + (mm(a[0], b[1], dims) + mm(a[1], b[0], dims))


def kernel(
    n_sub,
    n_grp,
    count_ref,
    coup_ref,
    basis_ref,
    cmap_ref,
    rzp_ref,
    schur_h,
    linv_h,
    diag_h,
    chain_h,
    res_h,
    dir_h,
    upd_h,
    new_h,
    sv,
    iv,
    dv,
    lv,
    rv,
    pv,
    rhi,
    xhi,
    xlo,
    lp,
    ulp,
    ud,
    bt,
    wcat,
    btedge,
    kown,
    knext,
    mapv,
    tsend,
    trecv,
    rsend,
    rrecv,
    asend,
    arecv,
    amat,
    lmat,
    fmat,
    e0v,
    bv,
    brecv,
    bpl,
    yin,
    yout,
    y0v,
    y1v,
    qsend,
    qrecv,
    tin,
    tout,
    csend,
    crecv,
    cbuf,
    chalo,
    dhalo,
    lhalo,
    bhalo,
    clv,
    gmat,
    mmat,
    sums,
    gath1,
    mid,
    gath2,
    load_sem,
    out_sem,
    t_sem,
    r_sem,
    a_sem,
    b_sem,
    y_sem,
    q_sem,
    ti_sem,
    c_sem,
    ch_sem,
    dh_sem,
    lh_sem,
    bh_sem,
    kn_sem,
    s1_sem,
    s2_sem,
):
    s = lax.axis_index("sub")
    g = lax.axis_index("grp")
    odd = lax.rem(g, 2) == 1
    even = jnp.logical_not(odd)
    plane = g // 2
    n_plane = n_grp // 2
    first_plane = plane == 0
    last_plane = plane == n_plane - 1
    faces, cols = rv.shape[1], rv.shape[2]
    share = coup_ref.shape[1]
    slots = basis_ref.shape[1]
    blk = dv.shape[1]
    part = cols // n_sub
    wide = n_sub * LANE
    me = s * n_grp + g
    has_prev = me > 0
    has_next = me < n_sub * n_grp - 1
    prev_at = {"sub": jnp.where(g > 0, s, s - 1), "grp": jnp.where(g > 0, g - 1, n_grp - 1)}
    next_at = {
        "sub": jnp.where(g < n_grp - 1, s, s + 1),
        "grp": jnp.where(g < n_grp - 1, g + 1, 0),
    }
    pair_at = {"grp": jnp.where(odd, g - 1, g + 1)}

    def remote(src, dst, sems, k, where):
        return pltpu.make_async_remote_copy(
            src_ref=src,
            dst_ref=dst,
            send_sem=sems.at[0, k],
            recv_sem=sems.at[1, k],
            device_id=where,
            device_id_type=pl.DeviceIdType.MESH,
        )

    def load(src, dst, k):
        return pltpu.make_async_copy(src, dst, load_sem.at[k])

    ld_r = [load(res_h.at[j], rv.at[j], j) for j in range(2)]
    ld_l = load(chain_h, lv, 2)
    ld_d = load(diag_h, dv, 3)
    ld_i = load(linv_h, iv, 4)
    ld_p = load(dir_h, pv, 5)
    ld_s = load(schur_h, sv, 6)
    for c in ld_r + [ld_l, ld_d, ld_i, ld_p, ld_s]:
        c.start()

    barrier = pltpu.get_barrier_semaphore()
    for k in range(1, n_sub):
        pl.semaphore_signal(
            barrier, inc=1, device_id={"sub": lax.rem(s + k, n_sub)},
            device_id_type=pl.DeviceIdType.MESH,
        )
    for k in range(1, n_grp):
        pl.semaphore_signal(
            barrier, inc=1, device_id={"grp": lax.rem(g + k, n_grp)},
            device_id_type=pl.DeviceIdType.MESH,
        )
    wrap_prev = jnp.logical_and(g == 0, s > 0)
    wrap_next = jnp.logical_and(g == n_grp - 1, s < n_sub - 1)

    @pl.when(wrap_prev)
    def _():
        pl.semaphore_signal(
            barrier, inc=1, device_id=prev_at, device_id_type=pl.DeviceIdType.MESH
        )

    @pl.when(wrap_next)
    def _():
        pl.semaphore_signal(
            barrier, inc=1, device_id=next_at, device_id_type=pl.DeviceIdType.MESH
        )

    mapv[...] = jnp.zeros_like(mapv)
    mapv[0:2, 0:slots] = cmap_ref[...]
    lane = lax.broadcasted_iota(jnp.int32, (1, LANE), 1)
    one = jnp.where(lane < count_ref[0], mapv[0:1, :], -1).astype(F32)
    two = jnp.where(lane < count_ref[1], mapv[1:2, :], -1).astype(F32)
    two = pltpu.roll(jnp.broadcast_to(two, (8, LANE)), slots, 1)[0:1, :]
    row = jnp.where(lane < slots, one, jnp.where(lane < 2 * slots, two, -1.0))
    tsend[...] = jnp.broadcast_to(row, tsend.shape)
    trecv[s] = jnp.broadcast_to(row, tsend.shape)

    b0 = basis_ref[0].astype(F32)
    b1 = basis_ref[1].astype(F32)
    zb = jnp.zeros_like(b0)
    bs = [jnp.concatenate([b0, zb], 0).astype(BF16), jnp.concatenate([zb, b1], 0).astype(BF16)]

    cl = jnp.zeros((2 * slots, cols), F32)
    for j in range(2):
        ld_r[j].wait()
        hi, lo = split(rv[j])
        rhi[j] = hi
        cl = cl + (mm(bs[j], hi) + mm(bs[j], lo))
    clv[...] = cl
    clt = jnp.concatenate([cl, jnp.zeros((LANE - 2 * slots, cols), F32)], 0).T
    for q in range(n_sub):
        rsend[q] = clt[q * part:(q + 1) * part, :]
    rrecv[s] = rsend[s]

    extra = jnp.where(wrap_prev, 1, 0) + jnp.where(wrap_next, 1, 0)
    pl.semaphore_wait(barrier, n_sub - 1 + n_grp - 1 + extra)

    sub_at = [{"sub": lax.rem(s + k, n_sub)} for k in range(n_sub)]
    sub_in = [lax.rem(s + n_sub - k, n_sub) for k in range(n_sub)]
    t_copy = [remote(tsend, trecv.at[s], t_sem, k, sub_at[k]) for k in range(1, n_sub)]
    r_copy = [
        remote(rsend.at[lax.rem(s + k, n_sub)], rrecv.at[s], r_sem, k, sub_at[k])
        for k in range(1, n_sub)
    ]
    for c in t_copy:
        c.start()
    for c in r_copy:
        c.start()

    ld_l.wait()
    lone = [split(lv[j]) for j in range(2)]
    for j in range(2):
        lmat[2 * j], lmat[2 * j + 1] = lone[j]
    a_own = mm3(lone[1], lone[0])
    asend[...] = a_own
    a_copy = remote(asend, arecv, a_sem, 0, pair_at)
    a_copy.start()

    btall = jnp.concatenate([b0, b1, jnp.zeros((LANE - 2 * slots, faces), F32)], 0).T
    lane_f = lax.broadcasted_iota(jnp.int32, btall.shape, 1)
    bt0 = jnp.where(lane_f < slots, btall, 0.0)
    bt1 = jnp.where(lane_f < slots, 0.0, btall)
    bt[0] = bt0.astype(BF16)
    bt[1] = bt1.astype(BF16)
    btedge[0] = bt0[0:share]
    btedge[1] = bt1[faces - share:]
    for j in range(2):
        kown[j] = jnp.broadcast_to(coup_ref[j:j + 1, :], (LANE, share)).T

    ld_p.wait()
    d_next = remote(pv.at[1, pl.ds(faces - share, share)], dhalo.at[0], dh_sem, 0, next_at)
    d_prev = remote(pv.at[0, pl.ds(0, share)], dhalo.at[1], dh_sem, 1, prev_at)
    l_next = remote(lp.at[1, pl.ds(faces - share, share)], lhalo.at[0], lh_sem, 0, next_at)
    l_prev = remote(lp.at[0, pl.ds(0, share)], lhalo.at[1], lh_sem, 1, prev_at)
    b_next = remote(btedge.at[1], bhalo.at[0], bh_sem, 0, next_at)
    b_prev = remote(btedge.at[0], bhalo.at[1], bh_sem, 1, prev_at)
    k_prev = remote(kown.at[0], knext, kn_sem, 0, prev_at)
    c_next = remote(cbuf.at[pl.ds(slots, slots)], chalo.at[0], ch_sem, 0, next_at)
    c_prev = remote(cbuf.at[pl.ds(0, slots)], chalo.at[1], ch_sem, 1, prev_at)

    @pl.when(has_next)
    def _():
        b_next.start()
        d_next.start()

    @pl.when(has_prev)
    def _():
        b_prev.start()
        k_prev.start()
        d_prev.start()

    @pl.when(jnp.logical_not(has_prev))
    def _():
        dhalo[0] = jnp.zeros_like(dhalo[0])
        lhalo[0] = jnp.zeros_like(lhalo[0])
        bhalo[0] = jnp.zeros_like(bhalo[0])
        chalo[0] = jnp.zeros_like(chalo[0])

    @pl.when(jnp.logical_not(has_next))
    def _():
        dhalo[1] = jnp.zeros_like(dhalo[1])
        lhalo[1] = jnp.zeros_like(lhalo[1])
        bhalo[1] = jnp.zeros_like(bhalo[1])
        chalo[1] = jnp.zeros_like(chalo[1])
        knext[...] = jnp.zeros_like(knext)

    ld_d.wait()
    for k in range(1, n_sub):
        t_copy[k - 1].wait()
    trow = jnp.concatenate([trecv[q][0:1, :] for q in range(n_sub)], 1)
    rows = lax.broadcasted_iota(jnp.int32, (blk, wide), 0).astype(F32)
    fs = []
    for j in range(2):
        sel = (rows + float(blk * j) == trow).astype(F32).astype(BF16)
        dhi, dlo = split(dv[j])
        fs.append(mm(dhi, sel) + mm(dlo, sel))
    f_pair = [split(fs[0]), split(fs[1])]
    for j in range(2):
        fmat[2 * j], fmat[2 * j + 1] = f_pair[j]
    hb = split(fs[1] - mm3(lone[1], f_pair[0]))

    for k in range(1, n_sub):
        r_copy[k - 1].wait()
    rcat = split(jnp.concatenate([rrecv[q] for q in range(n_sub)], 1))
    b_val = mm3(rcat, hb, NT)
    bv[...] = b_val
    b_copy = remote(bv, brecv, b_sem, 0, pair_at)

    @pl.when(even)
    def _():
        b_copy.start()

    e0v[...] = mm3(rcat, f_pair[0], NT)
    a_copy.wait()
    a_oth = arecv[...]
    a0 = jnp.where(odd, a_oth, a_own)
    a1 = jnp.where(odd, a_own, a_oth)
    a0p, a1p = split(a0), split(a1)
    app = split(mm3(a1p, a0p))
    amat[0], amat[1] = a0p
    amat[2], amat[3] = a1p
    amat[4], amat[5] = app

    def a_of(k):
        return amat[2 * k], amat[2 * k + 1]

    def l_of(k):
        return lmat[2 * k], lmat[2 * k + 1]

    def heavy():
        ld_i.wait()

        def local(c, _):
            at = pl.ds(pl.multiple_of(c * CHUNK, CHUNK), CHUNK)
            for j in range(2):
                lp[j, at, :] = mm(iv[j, at, :], rhi[j])
            return 0

        lax.fori_loop(0, faces // CHUNK, local, 0)

        @pl.when(has_next)
        def _():
            l_next.start()

        @pl.when(has_prev)
        def _():
            l_prev.start()

        ld_s.wait()
        for j in range(2):
            for src, dst in ((pv, ud), (lp, ulp)):
                hi, lo = split(src[j])
                xhi[...] = hi
                xlo[...] = lo

                def apply(c, _, dst=dst, j=j):
                    at = pl.ds(pl.multiple_of(c * CHUNK, CHUNK), CHUNK)
                    block = sv[j, at, :]
                    dst[j, at, :] = mm(block, xhi[...]) + mm(block, xlo[...])
                    return 0

                lax.fori_loop(0, faces // CHUNK, apply, 0)

            hi_lane = j

            def wide_basis(c, _, j=hi_lane):
                at = pl.ds(pl.multiple_of(c * CHUNK, CHUNK), CHUNK)
                w = mm(sv[j, at, :], bt[j])
                whi, wlo = split(w)
                wcat[j, at, 0:LANE] = whi
                wcat[j, at, LANE:2 * LANE] = wlo
                wcat[j, at, 2 * LANE:3 * LANE] = whi
                return 0

            lax.fori_loop(0, faces // CHUNK, wide_basis, 0)

    late = plane >= n_plane // 2

    @pl.when(late)
    def _():
        heavy()

    up = {"grp": 2 * plane + 3}
    up_even = {"grp": 2 * plane + 2}
    down = {"grp": 2 * plane - 2}
    down_odd = {"grp": 2 * plane - 1}
    y_odd = remote(yout, yin, y_sem, 0, up)
    y_even = remote(yout, yin, y_sem, 1, up_even)
    q_copy = remote(qsend, qrecv, q_sem, 0, pair_at)
    t_even = remote(tout, tin, ti_sem, 0, down)
    t_odd = remote(tout, tin, ti_sem, 1, down_odd)

    @pl.when(first_plane)
    def _():
        yin[...] = jnp.zeros_like(yin)

    @pl.when(last_plane)
    def _():
        tin[...] = jnp.zeros_like(tin)

    @pl.when(odd)
    def _():
        b_copy.wait_recv()
        first = brecv[...]
        bpl[...] = bv[...] + mm3(split(first), a_of(1), NT)

        @pl.when(jnp.logical_not(first_plane))
        def _():
            y_odd.wait_recv()

        before = split(yin[...])
        after = bpl[...] + mm3(before, a_of(2), NT)
        yout[...] = after

        @pl.when(jnp.logical_not(last_plane))
        def _():
            y_odd.start()
            y_even.start()

        middle = first + mm3(before, a_of(0), NT)
        y0 = e0v[...] - mm3(split(middle), l_of(0), NT)
        y0v[...] = y0
        y1v[...] = after
        qsend[...] = mm3(split(y0), l_of(0)) - mm3(split(after), a_of(1))
        q_copy.start()

    @pl.when(even)
    def _():
        @pl.when(jnp.logical_not(first_plane))
        def _():
            y_even.wait_recv()

        before = split(yin[...])
        y0 = e0v[...] - mm3(before, l_of(0), NT)
        y1 = bv[...] + mm3(before, a_of(0), NT)
        y0v[...] = y0
        y1v[...] = y1
        bpl[...] = mm3(split(y0), l_of(0)) - mm3(split(y1), a_of(0))

    @pl.when(jnp.logical_not(late))
    def _():
        heavy()

    @pl.when(even)
    def _():
        q_copy.wait_recv()
        q1 = qrecv[...]
        bpl[...] = bpl[...] + mm3(split(q1), a_of(0))

        @pl.when(jnp.logical_not(last_plane))
        def _():
            t_even.wait_recv()

        after = split(tin[...])
        tout[...] = bpl[...] + mm3(after, a_of(2))

        @pl.when(jnp.logical_not(first_plane))
        def _():
            t_even.start()
            t_odd.start()

        y1v[...] = y1v[...] - (q1 + mm3(after, a_of(1)))

    @pl.when(odd)
    def _():
        @pl.when(jnp.logical_not(last_plane))
        def _():
            t_odd.wait_recv()

        y1v[...] = y1v[...] - tin[...]

    w1 = split(y1v[...])
    w0 = split(y0v[...] - mm3(w1, l_of(1)))
    call = mm3(w0, (fmat[0], fmat[1])) + mm3(w1, (fmat[2], fmat[3]))
    for q in range(n_sub):
        csend[q] = call[:, q * LANE:(q + 1) * LANE]
    crecv[s] = csend[s]
    c_copy = [
        remote(csend.at[lax.rem(s + k, n_sub)], crecv.at[s], c_sem, k, sub_at[k])
        for k in range(1, n_sub)
    ]
    for c in c_copy:
        c.start()

    @pl.when(has_prev)
    def _():
        d_next.wait_recv()
        l_next.wait_recv()
        b_next.wait_recv()

    @pl.when(has_next)
    def _():
        d_prev.wait_recv()
        l_prev.wait_recv()
        b_prev.wait_recv()
        k_prev.wait_recv()

    def spread(k):
        return jnp.concatenate([k] * (cols // LANE), 1)

    k0, k1, k2 = spread(kown[0]), spread(kown[1]), spread(knext[...])
    head, tail = pl.ds(0, share), pl.ds(faces - share, share)
    for src, dst, halo in ((pv, ud, dhalo), (lp, ulp, lhalo)):
        dst[0, head, :] = dst[0, head, :] - k0 * halo[0]
        dst[0, tail, :] = dst[0, tail, :] - k1 * src[1, head, :]
        dst[1, head, :] = dst[1, head, :] - k1 * src[0, tail, :]
        dst[1, tail, :] = dst[1, tail, :] - k2 * halo[1]
    for j, at, value in (
        (0, tail, bt[1, head, :]),
        (1, head, bt[0, tail, :]),
    ):
        w = wcat[j, at, 0:LANE].astype(F32) + wcat[j, at, LANE:2 * LANE].astype(F32)
        whi, wlo = split(w - kown[1] * value.astype(F32))
        wcat[j, at, 0:LANE] = whi
        wcat[j, at, LANE:2 * LANE] = wlo
        wcat[j, at, 2 * LANE:3 * LANE] = whi
    edge0 = split(kown[0] * bhalo[0])
    edge1 = split(knext[...] * bhalo[1])
    mx = (mm(bs[0][:, 0:share], edge0[0]) + mm(bs[0][:, 0:share], edge0[1])) + (
        mm(bs[1][:, faces - share:], edge1[0]) + mm(bs[1][:, faces - share:], edge1[1])
    )
    m_own = jnp.zeros((2 * slots, LANE), F32)
    g1 = jnp.zeros((2 * slots, cols), F32)
    g3 = jnp.zeros((2 * slots, cols), F32)
    for j in range(2):
        m_own = m_own + (mm(bs[j], wcat[j, :, 0:LANE]) + mm(bs[j], wcat[j, :, LANE:2 * LANE]))
        hi, lo = split(ulp[j])
        g1 = g1 + (mm(bs[j], hi) + mm(bs[j], lo))
        hi, lo = split(ud[j])
        g3 = g3 + (mm(bs[j], hi) + mm(bs[j], lo))
    acc = [jnp.zeros((8, cols), F32) for _ in range(4)]

    def dots(c, acc):
        at = pl.ds(pl.multiple_of(c * LANE, LANE), LANE)
        acc = list(acc)
        for j in range(2):
            l, p, ul, u, r = lp[j, at, :], pv[j, at, :], ulp[j, at, :], ud[j, at, :], rv[j, at, :]
            for i, x in enumerate((r * l, l * ul, l * u, p * u)):
                acc[i] = acc[i] + jnp.sum(x.reshape(LANE // 8, 8, cols), 0)
        return tuple(acc)

    acc = lax.fori_loop(0, faces // LANE, dots, tuple(acc))
    base = [jnp.sum(x, 0, keepdims=True) for x in acc]

    for c in c_copy:
        c.wait()
    corr = jnp.concatenate([crecv[q] for q in range(n_sub)], 0).T
    cbuf[...] = corr[0:2 * slots]

    @pl.when(has_next)
    def _():
        c_next.start()

    @pl.when(has_prev)
    def _():
        c_prev.start()

    chi, clo = split(corr)
    own = corr[0:2 * slots]
    mhi, mlo = split(m_own)
    mc = mm3((mhi, mlo), (chi, clo))

    @pl.when(has_prev)
    def _():
        c_next.wait_recv()

    @pl.when(has_next)
    def _():
        c_prev.wait_recv()

    cx = jnp.concatenate([chalo[1], chalo[0], jnp.zeros((LANE - 2 * slots, cols), F32)], 0)
    cxp = split(cx)
    mc = mc - mm3(split(mx), cxp)
    rz = base[0] + jnp.sum(clv[...] * own, 0, keepdims=True)
    qa = base[1] + jnp.sum(own * (2.0 * g1 + mc), 0, keepdims=True)
    qb = 2.0 * (base[2] + jnp.sum(own * g3, 0, keepdims=True))
    sums[...] = jnp.concatenate([rz, qa, qb, base[3], jnp.zeros((4, cols), F32)], 0)
    gath1[s] = sums[...]
    s1 = [remote(sums, gath1.at[s], s1_sem, k, sub_at[k]) for k in range(1, n_sub)]
    for c in s1:
        c.start()

    c2 = jnp.concatenate([chi, clo], 0)
    c3 = jnp.concatenate([chi, chi, clo], 0)

    def finish(j):
        def step(c, _):
            at = pl.ds(pl.multiple_of(c * CHUNK, CHUNK), CHUNK)
            block = bt[j, at, :]
            lp[j, at, :] = lp[j, at, :] + mm(jnp.concatenate([block, block], 1), c2)
            ulp[j, at, :] = ulp[j, at, :] + mm(wcat[j, at, :], c3)
            return 0

        lax.fori_loop(0, faces // CHUNK, step, 0)

    if True:
        @pl.when(has_next)
        def _():
            l_next.wait_send()

        @pl.when(has_prev)
        def _():
            l_prev.wait_send()

    for c in s1:
        c.wait()
    total = gath1[0]
    for q in range(1, n_sub):
        total = total + gath1[q]
    mid[...] = total
    gath2[g] = total
    s2 = [
        remote(mid, gath2.at[g], s2_sem, k, {"grp": lax.rem(g + k, n_grp)})
        for k in range(1, n_grp)
    ]
    for c in s2:
        c.start()
    finish(0)
    finish(1)
    ulp[0, head, :] = ulp[0, head, :] - mm3(edge0, cxp)
    ulp[1, tail, :] = ulp[1, tail, :] - mm3(edge1, cxp)
    for c in s2:
        c.wait()
    total = gath2[0]
    for q in range(1, n_grp):
        total = total + gath2[q]
    rz = total[0:1]
    beta = rz / rzp_ref[...]
    step_size = rz / (total[1:2] + beta * (total[2:3] + beta * total[3:4]))

    @pl.when(has_next)
    def _():
        d_next.wait_send()
        b_next.wait_send()
        c_next.wait_send()

    @pl.when(has_prev)
    def _():
        d_prev.wait_send()
        b_prev.wait_send()
        k_prev.wait_send()
        c_prev.wait_send()

    out = []
    for j in range(2):
        for h in range(faces // CHUNK):
            at = pl.ds(h * CHUNK, CHUNK)
            n = j * (faces // CHUNK) + h
            lp[j, at, :] = step_size * (lp[j, at, :] + beta * pv[j, at, :])
            cu = pltpu.make_async_copy(lp.at[j, at], upd_h.at[j, at], out_sem.at[0, n])
            cu.start()
            ulp[j, at, :] = rv[j, at, :] - step_size * (ulp[j, at, :] + beta * ud[j, at, :])
            cn = pltpu.make_async_copy(ulp.at[j, at], new_h.at[j, at], out_sem.at[1, n])
            cn.start()
            out += [cu, cn]

    @pl.when(even)
    def _():
        b_copy.wait_send()

        @pl.when(jnp.logical_not(first_plane))
        def _():
            t_even.wait_send()
            t_odd.wait_send()

    @pl.when(odd)
    def _():
        q_copy.wait_send()

        @pl.when(jnp.logical_not(last_plane))
        def _():
            y_odd.wait_send()
            y_even.wait_send()

    for c in out:
        c.wait()


def shards(
    schur,
    local_inverse,
    coupling,
    basis,
    coarse_map,
    coarse_count,
    diag_inverse,
    chain_factor,
    residual,
    direction,
    rz_prev,
):
    n_sub, n_grp = lax.axis_size("sub"), lax.axis_size("grp")
    subs, faces, cols = residual.shape
    share = coupling.shape[1]
    slots = basis.shape[1]
    blk = diag_inverse.shape[1]
    part = cols // n_sub
    wide = n_sub * LANE
    vm = pltpu.VMEM
    dma = pltpu.SemaphoreType.DMA
    whole = pl.BlockSpec(memory_space=pltpu.VMEM)
    far = pl.BlockSpec(memory_space=pl.ANY)
    strip = vm((part, blk), F32)
    scratch = [
        vm(schur.shape, BF16),
        vm(schur.shape, BF16),
        vm(diag_inverse.shape, F32),
        vm(chain_factor.shape, F32),
        vm(residual.shape, F32),
        vm(residual.shape, F32),
        vm(residual.shape, BF16),
        vm((faces, cols), BF16),
        vm((faces, cols), BF16),
        vm(residual.shape, F32),
        vm(residual.shape, F32),
        vm(residual.shape, F32),
        vm((subs, faces, LANE), BF16),
        vm((subs, faces, 3 * LANE), BF16),
        vm((2, share, LANE), F32),
        vm((2, share, LANE), F32),
        vm((share, LANE), F32),
        vm((8, LANE), jnp.int32),
        vm((8, LANE), F32),
        vm((n_sub, 8, LANE), F32),
        vm((n_sub, part, LANE), F32),
        vm((n_sub, part, LANE), F32),
        vm((blk, blk), F32),
        vm((blk, blk), F32),
        vm((6, blk, blk), BF16),
        vm((4, blk, blk), BF16),
        vm((4, blk, wide), BF16),
        strip,
        strip,
        strip,
        strip,
        strip,
        strip,
        strip,
        strip,
        strip,
        strip,
        strip,
        strip,
        vm((n_sub, part, LANE), F32),
        vm((n_sub, part, LANE), F32),
        vm((2 * slots, cols), F32),
        vm((2, slots, cols), F32),
        vm((2, share, cols), F32),
        vm((2, share, cols), F32),
        vm((2, share, LANE), F32),
        vm((2 * slots, cols), F32),
        vm((8, LANE), F32),
        vm((8, LANE), F32),
        vm((8, cols), F32),
        vm((n_sub, 8, cols), F32),
        vm((8, cols), F32),
        vm((n_grp, 8, cols), F32),
        dma((7,)),
        dma((2, 2 * (faces // CHUNK))),
        dma((2, n_sub)),
        dma((2, n_sub)),
        dma((2, 1)),
        dma((2, 1)),
        dma((2, 2)),
        dma((2, 1)),
        dma((2, 2)),
        dma((2, n_sub)),
        dma((2, 2)),
        dma((2, 2)),
        dma((2, 2)),
        dma((2, 2)),
        dma((2, 1)),
        dma((2, n_sub)),
        dma((2, n_grp)),
    ]
    return pl.pallas_call(
        functools.partial(kernel, n_sub, n_grp),
        out_shape=(
            jax.ShapeDtypeStruct(residual.shape, F32),
            jax.ShapeDtypeStruct(residual.shape, F32),
        ),
        in_specs=[pl.BlockSpec(memory_space=pltpu.SMEM)] + [whole] * 4 + [far] * 6,
        out_specs=(far, far),
        scratch_shapes=scratch,
        compiler_params=pltpu.CompilerParams(
            collective_id=0, has_side_effects=True, vmem_limit_bytes=60 * 2**20
        ),
    )(
        coarse_count,
        coupling,
        basis,
        coarse_map,
        rz_prev[None, :],
        schur,
        local_inverse,
        diag_inverse,
        chain_factor,
        residual,
        direction,
    )


def solution(mesh):
    return jax.shard_map(
        shards,
        mesh=mesh,
        in_specs=(
            P(("sub", "grp"), None, None),
            P(("sub", "grp"), None, None),
            P(("sub", "grp"), None),
            P(("sub", "grp"), None, None),
            P(("sub", "grp"), None),
            P(("sub", "grp")),
            P("grp", None, None),
            P("grp", None, None),
            P(("sub", "grp"), None, None),
            P(("sub", "grp"), None, None),
            P(),
        ),
        out_specs=(P(("sub", "grp"), None, None), P(("sub", "grp"), None, None)),
        check_vma=False,
    )
```

```python
import functools

import jax
import jax.numpy as jnp
from jax import lax
from jax.experimental import pallas as pl
from jax.experimental.pallas import tpu as pltpu
from jax.sharding import PartitionSpec as P

F32 = jnp.float32
BF16 = jnp.bfloat16
NN = (((1,), (0,)), ((), ()))
NT = (((1,), (1,)), ((), ()))
LANE = 128
CHUNK = 256


def mm(a, b, dims=NN):
    return lax.dot_general(a, b, dims, preferred_element_type=F32)


def split(x):
    hi = x.astype(BF16)
    return hi, (x - hi.astype(F32)).astype(BF16)


def mm3(a, b, dims=NN):
    return mm(a[0], b[0], dims) + (mm(a[0], b[1], dims) + mm(a[1], b[0], dims))


def kernel(
    n_sub,
    n_grp,
    count_ref,
    coup_ref,
    basis_ref,
    cmap_ref,
    schur_h,
    linv_h,
    diag_h,
    chain_h,
    res_h,
    dir_h,
    p_h,
    up_h,
    ud_h,
    sums_out,
    sv,
    iv,
    dv,
    lv,
    rv,
    pv,
    rhi,
    xhi,
    xlo,
    lp,
    ulp,
    ud,
    bt,
    wcat,
    bsend,
    kown,
    mapv,
    tsend,
    trecv,
    rsend,
    rrecv,
    asend,
    arecv,
    amat,
    lmat,
    fmat,
    e0v,
    bv,
    brecv,
    bpl,
    yin,
    yout,
    y0v,
    y1v,
    qsend,
    qrecv,
    tin,
    tout,
    csend,
    crecv,
    cbuf,
    chalo,
    dhalo,
    lhalo,
    bhalo,
    clv,
    sums,
    gath1,
    mid,
    gath2,
    load_sem,
    out_sem,
    t_sem,
    r_sem,
    a_sem,
    b_sem,
    y_sem,
    q_sem,
    ti_sem,
    c_sem,
    ch_sem,
    dh_sem,
    lh_sem,
    bh_sem,
    s1_sem,
    s2_sem,
):
    s = lax.axis_index("sub")
    g = lax.axis_index("grp")
    odd = lax.rem(g, 2) == 1
    even = jnp.logical_not(odd)
    plane = g // 2
    n_plane = n_grp // 2
    first_plane = plane == 0
    last_plane = plane == n_plane - 1
    faces, cols = rv.shape[1], rv.shape[2]
    share = coup_ref.shape[1]
    slots = basis_ref.shape[1]
    blk = dv.shape[1]
    part = cols // n_sub
    wide = n_sub * LANE
    me = s * n_grp + g
    has_prev = me > 0
    has_next = me < n_sub * n_grp - 1
    prev_at = {"sub": jnp.where(g > 0, s, s - 1), "grp": jnp.where(g > 0, g - 1, n_grp - 1)}
    next_at = {
        "sub": jnp.where(g < n_grp - 1, s, s + 1),
        "grp": jnp.where(g < n_grp - 1, g + 1, 0),
    }
    pair_at = {"grp": jnp.where(odd, g - 1, g + 1)}

    def remote(src, dst, sems, k, where):
        return pltpu.make_async_remote_copy(
            src_ref=src,
            dst_ref=dst,
            send_sem=sems.at[0, k],
            recv_sem=sems.at[1, k],
            device_id=where,
            device_id_type=pl.DeviceIdType.MESH,
        )

    def load(src, dst, k):
        return pltpu.make_async_copy(src, dst, load_sem.at[k])

    ld_r = [load(res_h.at[j], rv.at[j], j) for j in range(2)]
    ld_l = load(chain_h, lv, 2)
    ld_d = load(diag_h, dv, 3)
    ld_i = load(linv_h, iv, 4)
    ld_p = load(dir_h, pv, 5)
    ld_s = load(schur_h, sv, 6)
    for c in ld_r + [ld_l, ld_d, ld_i, ld_p, ld_s]:
        c.start()

    barrier = pltpu.get_barrier_semaphore()
    for k in range(1, n_sub):
        pl.semaphore_signal(
            barrier, inc=1, device_id={"sub": lax.rem(s + k, n_sub)},
            device_id_type=pl.DeviceIdType.MESH,
        )
    for k in range(1, n_grp):
        pl.semaphore_signal(
            barrier, inc=1, device_id={"grp": lax.rem(g + k, n_grp)},
            device_id_type=pl.DeviceIdType.MESH,
        )
    wrap_prev = jnp.logical_and(g == 0, s > 0)
    wrap_next = jnp.logical_and(g == n_grp - 1, s < n_sub - 1)

    @pl.when(wrap_prev)
    def _():
        pl.semaphore_signal(
            barrier, inc=1, device_id=prev_at, device_id_type=pl.DeviceIdType.MESH
        )

    @pl.when(wrap_next)
    def _():
        pl.semaphore_signal(
            barrier, inc=1, device_id=next_at, device_id_type=pl.DeviceIdType.MESH
        )

    b0 = basis_ref[0].astype(F32)
    b1 = basis_ref[1].astype(F32)
    zb = jnp.zeros_like(b0)
    bs = [jnp.concatenate([b0, zb], 0).astype(BF16), jnp.concatenate([zb, b1], 0).astype(BF16)]
    crow = jnp.broadcast_to(coup_ref[0:1, :], (8, share))
    bsend[0] = jnp.concatenate([b0[:, 0:share], crow], 0)
    bsend[1] = jnp.concatenate([b1[:, faces - share:], crow], 0)

    d_next = remote(dir_h.at[1, pl.ds(faces - share, share)], dhalo.at[0], dh_sem, 0, next_at)
    d_prev = remote(dir_h.at[0, pl.ds(0, share)], dhalo.at[1], dh_sem, 1, prev_at)
    l_next = remote(lp.at[1, pl.ds(faces - share, share)], lhalo.at[0], lh_sem, 0, next_at)
    l_prev = remote(lp.at[0, pl.ds(0, share)], lhalo.at[1], lh_sem, 1, prev_at)
    b_next = remote(bsend.at[1], bhalo.at[0], bh_sem, 0, next_at)
    b_prev = remote(bsend.at[0], bhalo.at[1], bh_sem, 1, prev_at)
    c_next = remote(cbuf.at[pl.ds(slots, slots)], chalo.at[0], ch_sem, 0, next_at)
    c_prev = remote(cbuf.at[pl.ds(0, slots)], chalo.at[1], ch_sem, 1, prev_at)
    extra = jnp.where(wrap_prev, 1, 0) + jnp.where(wrap_next, 1, 0)
    pl.semaphore_wait(barrier, n_sub - 1 + n_grp - 1 + extra)

    mapv[...] = jnp.zeros_like(mapv)
    mapv[0:2, 0:slots] = cmap_ref[...]
    lane = lax.broadcasted_iota(jnp.int32, (1, LANE), 1)
    one = jnp.where(lane < count_ref[0], mapv[0:1, :], -1).astype(F32)
    two = jnp.where(lane < count_ref[1], mapv[1:2, :], -1).astype(F32)
    two = pltpu.roll(jnp.broadcast_to(two, (8, LANE)), slots, 1)[0:1, :]
    row = jnp.where(lane < slots, one, jnp.where(lane < 2 * slots, two, -1.0))
    tsend[...] = jnp.broadcast_to(row, tsend.shape)
    trecv[s] = jnp.broadcast_to(row, tsend.shape)

    cl = jnp.zeros((2 * slots, cols), F32)
    for j in range(2):
        ld_r[j].wait()
        hi, lo = split(rv[j])
        rhi[j] = hi
        cl = cl + (mm(bs[j], hi) + mm(bs[j], lo))
    clv[...] = cl
    clt = jnp.concatenate([cl, jnp.zeros((LANE - 2 * slots, cols), F32)], 0).T
    for q in range(n_sub):
        rsend[q] = clt[q * part:(q + 1) * part, :]
    rrecv[s] = rsend[s]

    sub_at = [{"sub": lax.rem(s + k, n_sub)} for k in range(n_sub)]
    sub_in = [lax.rem(s + n_sub - k, n_sub) for k in range(n_sub)]
    t_copy = [remote(tsend, trecv.at[s], t_sem, k, sub_at[k]) for k in range(1, n_sub)]
    r_copy = [
        remote(rsend.at[lax.rem(s + k, n_sub)], rrecv.at[s], r_sem, k, sub_at[k])
        for k in range(1, n_sub)
    ]
    for c in t_copy:
        c.start()
    for c in r_copy:
        c.start()

    ld_l.wait()
    lone = [split(lv[j]) for j in range(2)]
    for j in range(2):
        lmat[2 * j], lmat[2 * j + 1] = lone[j]
    a_own = mm3(lone[1], lone[0])
    asend[...] = a_own
    a_copy = remote(asend, arecv, a_sem, 0, pair_at)
    a_copy.start()

    @pl.when(has_next)
    def _():
        b_next.start()

    @pl.when(has_prev)
    def _():
        b_prev.start()

    def send_direction():
        @pl.when(has_next)
        def _():
            d_next.start()

        @pl.when(has_prev)
        def _():
            d_prev.start()

    late = plane >= n_plane // 2

    @pl.when(late)
    def _():
        send_direction()

    btall = jnp.concatenate([b0, b1, jnp.zeros((LANE - 2 * slots, faces), F32)], 0).T
    lane_f = lax.broadcasted_iota(jnp.int32, btall.shape, 1)
    bt0 = jnp.where(lane_f < slots, btall, 0.0)
    bt1 = jnp.where(lane_f < slots, 0.0, btall)
    bt[0] = bt0.astype(BF16)
    bt[1] = bt1.astype(BF16)
    for j in range(2):
        kown[j] = jnp.broadcast_to(coup_ref[j:j + 1, :], (LANE, share)).T

    ld_p.wait()

    @pl.when(jnp.logical_not(has_prev))
    def _():
        dhalo[0] = jnp.zeros_like(dhalo[0])
        lhalo[0] = jnp.zeros_like(lhalo[0])
        bhalo[0] = jnp.zeros_like(bhalo[0])
        chalo[0] = jnp.zeros_like(chalo[0])

    @pl.when(jnp.logical_not(has_next))
    def _():
        dhalo[1] = jnp.zeros_like(dhalo[1])
        lhalo[1] = jnp.zeros_like(lhalo[1])
        bhalo[1] = jnp.zeros_like(bhalo[1])
        chalo[1] = jnp.zeros_like(chalo[1])

    ld_d.wait()
    for k in range(1, n_sub):
        t_copy[k - 1].wait()
    trow = jnp.concatenate([trecv[q][0:1, :] for q in range(n_sub)], 1)
    rows = lax.broadcasted_iota(jnp.int32, (blk, wide), 0).astype(F32)
    fs = []
    for j in range(2):
        sel = (rows + float(blk * j) == trow).astype(F32).astype(BF16)
        dhi, dlo = split(dv[j])
        fs.append(mm(dhi, sel) + mm(dlo, sel))
    f_pair = [split(fs[0]), split(fs[1])]
    for j in range(2):
        fmat[2 * j], fmat[2 * j + 1] = f_pair[j]
    hb = split(fs[1] - mm3(lone[1], f_pair[0]))

    for k in range(1, n_sub):
        r_copy[k - 1].wait()
    rcat = split(jnp.concatenate([rrecv[q] for q in range(n_sub)], 1))
    b_val = mm3(rcat, hb, NT)
    bv[...] = b_val
    b_copy = remote(bv, brecv, b_sem, 0, pair_at)

    @pl.when(even)
    def _():
        b_copy.start()

        @pl.when(jnp.logical_not(late))
        def _():
            send_direction()

    e0v[...] = mm3(rcat, f_pair[0], NT)
    a_copy.wait()
    a_oth = arecv[...]
    a0 = jnp.where(odd, a_oth, a_own)
    a1 = jnp.where(odd, a_own, a_oth)
    a0p, a1p = split(a0), split(a1)
    app = split(mm3(a1p, a0p))
    amat[0], amat[1] = a0p
    amat[2], amat[3] = a1p
    amat[4], amat[5] = app

    def a_of(k):
        return amat[2 * k], amat[2 * k + 1]

    def l_of(k):
        return lmat[2 * k], lmat[2 * k + 1]

    ld_i.wait()

    def local(c, _):
        at = pl.ds(pl.multiple_of(c * CHUNK, CHUNK), CHUNK)
        for j in range(2):
            lp[j, at, :] = mm(iv[j, at, :], rhi[j])
        return 0

    lax.fori_loop(0, faces // CHUNK, local, 0)

    def send_local():
        @pl.when(has_next)
        def _():
            l_next.start()

        @pl.when(has_prev)
        def _():
            l_prev.start()

    @pl.when(jnp.logical_or(even, last_plane))
    def _():
        send_local()

    half = faces // 2

    def heavy():
        ld_s.wait()
        for j in range(2):
            for src, dst in ((pv, ud), (lp, ulp)):
                hi, lo = split(src[j])
                xhi[...] = hi
                xlo[...] = lo

                def apply(c, _, dst=dst, j=j):
                    at = pl.ds(pl.multiple_of(c * half, half), half)
                    block = sv[j, at, :]
                    dst[j, at, :] = mm(block, xhi[...]) + mm(block, xlo[...])
                    return 0

                lax.fori_loop(0, faces // half, apply, 0)

            hi_lane = j

            def wide_basis(c, _, j=hi_lane):
                at = pl.ds(pl.multiple_of(c * CHUNK, CHUNK), CHUNK)
                w = mm(sv[j, at, :], bt[j])
                whi, wlo = split(w)
                wcat[j, at, 0:LANE] = whi
                wcat[j, at, LANE:2 * LANE] = wlo
                wcat[j, at, 2 * LANE:3 * LANE] = whi
                return 0

            lax.fori_loop(0, faces // CHUNK, wide_basis, 0)

    @pl.when(late)
    def _():
        heavy()

    up = {"grp": 2 * plane + 3}
    up_even = {"grp": 2 * plane + 2}
    down = {"grp": 2 * plane - 2}
    down_odd = {"grp": 2 * plane - 1}
    y_odd = remote(yout, yin, y_sem, 0, up)
    y_even = remote(yout, yin, y_sem, 1, up_even)
    q_copy = remote(qsend, qrecv, q_sem, 0, pair_at)
    t_even = remote(tout, tin, ti_sem, 0, down)
    t_odd = remote(tout, tin, ti_sem, 1, down_odd)

    @pl.when(first_plane)
    def _():
        yin[...] = jnp.zeros_like(yin)

    @pl.when(last_plane)
    def _():
        tin[...] = jnp.zeros_like(tin)

    @pl.when(odd)
    def _():
        b_copy.wait_recv()
        first = brecv[...]
        bpl[...] = bv[...] + mm3(split(first), a_of(1), NT)

        @pl.when(jnp.logical_not(first_plane))
        def _():
            y_odd.wait_recv()

        before = split(yin[...])
        after = bpl[...] + mm3(before, a_of(2), NT)
        yout[...] = after

        @pl.when(jnp.logical_not(last_plane))
        def _():
            y_odd.start()
            y_even.start()

        middle = first + mm3(before, a_of(0), NT)
        y0 = e0v[...] - mm3(split(middle), l_of(0), NT)
        y0v[...] = y0
        y1v[...] = after
        qsend[...] = mm3(split(y0), l_of(0)) - mm3(split(after), a_of(1))
        q_copy.start()

        @pl.when(jnp.logical_not(late))
        def _():
            send_direction()

        @pl.when(jnp.logical_not(last_plane))
        def _():
            send_local()

    @pl.when(even)
    def _():
        @pl.when(jnp.logical_not(first_plane))
        def _():
            y_even.wait_recv()

        before = split(yin[...])
        y0 = e0v[...] - mm3(before, l_of(0), NT)
        y1 = bv[...] + mm3(before, a_of(0), NT)
        y0v[...] = y0
        y1v[...] = y1
        bpl[...] = mm3(split(y0), l_of(0)) - mm3(split(y1), a_of(0))

    @pl.when(jnp.logical_not(late))
    def _():
        heavy()

    @pl.when(even)
    def _():
        q_copy.wait_recv()
        q1 = qrecv[...]
        bpl[...] = bpl[...] + mm3(split(q1), a_of(0))

        @pl.when(jnp.logical_not(last_plane))
        def _():
            t_even.wait_recv()

        after = split(tin[...])
        tout[...] = bpl[...] + mm3(after, a_of(2))

        @pl.when(jnp.logical_not(first_plane))
        def _():
            t_even.start()
            t_odd.start()

        y1v[...] = y1v[...] - (q1 + mm3(after, a_of(1)))

    @pl.when(odd)
    def _():
        @pl.when(jnp.logical_not(last_plane))
        def _():
            t_odd.wait_recv()

        y1v[...] = y1v[...] - tin[...]

    w1 = split(y1v[...])
    w0 = split(y0v[...] - mm3(w1, l_of(1)))
    call = mm3(w0, (fmat[0], fmat[1])) + mm3(w1, (fmat[2], fmat[3]))
    for q in range(n_sub):
        csend[q] = call[:, q * LANE:(q + 1) * LANE]
    crecv[s] = csend[s]
    c_copy = [
        remote(csend.at[lax.rem(s + k, n_sub)], crecv.at[s], c_sem, k, sub_at[k])
        for k in range(1, n_sub)
    ]
    for c in c_copy:
        c.start()

    for c in c_copy:
        c.wait()
    corr = jnp.concatenate([crecv[q] for q in range(n_sub)], 0).T
    cbuf[...] = corr[0:2 * slots]

    @pl.when(has_next)
    def _():
        c_next.start()

    @pl.when(has_prev)
    def _():
        c_prev.start()

    @pl.when(has_prev)
    def _():
        d_next.wait_recv()
        l_next.wait_recv()
        b_next.wait_recv()

    @pl.when(has_next)
    def _():
        d_prev.wait_recv()
        l_prev.wait_recv()
        b_prev.wait_recv()

    def spread(k):
        return jnp.concatenate([k] * (cols // LANE), 1)

    gap = jnp.zeros((slots, share), F32)
    rest = jnp.zeros((LANE - 2 * slots, share), F32)
    bprev = jnp.concatenate([gap, bhalo[0][0:slots], rest], 0).T
    bnext = jnp.concatenate([bhalo[1][0:slots], gap, rest], 0).T
    knext = jnp.broadcast_to(bhalo[1][slots:slots + 1], (LANE, share)).T
    k0, k1, k2 = spread(kown[0]), spread(kown[1]), spread(knext)
    head, tail = pl.ds(0, share), pl.ds(faces - share, share)
    for src, dst, halo in ((pv, ud, dhalo), (lp, ulp, lhalo)):
        dst[0, head, :] = dst[0, head, :] - k0 * halo[0]
        dst[0, tail, :] = dst[0, tail, :] - k1 * src[1, head, :]
        dst[1, head, :] = dst[1, head, :] - k1 * src[0, tail, :]
        dst[1, tail, :] = dst[1, tail, :] - k2 * halo[1]
    for j, at, value in (
        (0, tail, bt[1, head, :]),
        (1, head, bt[0, tail, :]),
    ):
        w = wcat[j, at, 0:LANE].astype(F32) + wcat[j, at, LANE:2 * LANE].astype(F32)
        whi, wlo = split(w - kown[1] * value.astype(F32))
        wcat[j, at, 0:LANE] = whi
        wcat[j, at, LANE:2 * LANE] = wlo
        wcat[j, at, 2 * LANE:3 * LANE] = whi
    edge0 = split(kown[0] * bprev)
    edge1 = split(knext * bnext)
    mx = (mm(bs[0][:, 0:share], edge0[0]) + mm(bs[0][:, 0:share], edge0[1])) + (
        mm(bs[1][:, faces - share:], edge1[0]) + mm(bs[1][:, faces - share:], edge1[1])
    )
    m_own = jnp.zeros((2 * slots, LANE), F32)
    g1 = jnp.zeros((2 * slots, cols), F32)
    g3 = jnp.zeros((2 * slots, cols), F32)
    for j in range(2):
        m_own = m_own + (mm(bs[j], wcat[j, :, 0:LANE]) + mm(bs[j], wcat[j, :, LANE:2 * LANE]))
        hi, lo = split(ulp[j])
        g1 = g1 + (mm(bs[j], hi) + mm(bs[j], lo))
        hi, lo = split(ud[j])
        g3 = g3 + (mm(bs[j], hi) + mm(bs[j], lo))
    out_d = pltpu.make_async_copy(ud, ud_h, out_sem.at[4])
    out_d.start()
    acc = [jnp.zeros((8, cols), F32) for _ in range(4)]

    def dots(c, acc):
        at = pl.ds(pl.multiple_of(c * LANE, LANE), LANE)
        acc = list(acc)
        for j in range(2):
            l, p, ul, u, r = lp[j, at, :], pv[j, at, :], ulp[j, at, :], ud[j, at, :], rv[j, at, :]
            for i, x in enumerate((r * l, l * ul, l * u, p * u)):
                acc[i] = acc[i] + jnp.sum(x.reshape(LANE // 8, 8, cols), 0)
        return tuple(acc)

    acc = lax.fori_loop(0, faces // LANE, dots, tuple(acc))
    base = [jnp.sum(x, 0, keepdims=True) for x in acc]

    chi, clo = split(corr)
    own = corr[0:2 * slots]
    mhi, mlo = split(m_own)
    mc = mm3((mhi, mlo), (chi, clo))

    @pl.when(has_prev)
    def _():
        c_next.wait_recv()

    @pl.when(has_next)
    def _():
        c_prev.wait_recv()

    cx = jnp.concatenate([chalo[1], chalo[0], jnp.zeros((LANE - 2 * slots, cols), F32)], 0)
    cxp = split(cx)
    mc = mc - mm3(split(mx), cxp)
    rz = base[0] + jnp.sum(clv[...] * own, 0, keepdims=True)
    qa = base[1] + jnp.sum(own * (2.0 * g1 + mc), 0, keepdims=True)
    qb = 2.0 * (base[2] + jnp.sum(own * g3, 0, keepdims=True))
    sums[...] = jnp.concatenate([rz, qa, qb, base[3], jnp.zeros((4, cols), F32)], 0)
    gath1[s] = sums[...]
    s1 = [remote(sums, gath1.at[s], s1_sem, k, sub_at[k]) for k in range(1, n_sub)]
    for c in s1:
        c.start()

    c2 = jnp.concatenate([chi, clo], 0)
    c3 = jnp.concatenate([chi, chi, clo], 0)

    def finish(j):
        def step(c, _):
            at = pl.ds(pl.multiple_of(c * CHUNK, CHUNK), CHUNK)
            block = bt[j, at, :]
            lp[j, at, :] = lp[j, at, :] + mm(jnp.concatenate([block, block], 1), c2)
            ulp[j, at, :] = ulp[j, at, :] + mm(wcat[j, at, :], c3)
            return 0

        lax.fori_loop(0, faces // CHUNK, step, 0)

    if True:
        @pl.when(has_next)
        def _():
            l_next.wait_send()

        @pl.when(has_prev)
        def _():
            l_prev.wait_send()

    for c in s1:
        c.wait()
    total = gath1[0]
    for q in range(1, n_sub):
        total = total + gath1[q]
    mid[...] = total
    gath2[g] = total
    s2 = [
        remote(mid, gath2.at[g], s2_sem, k, {"grp": lax.rem(g + k, n_grp)})
        for k in range(1, n_grp)
    ]
    for c in s2:
        c.start()
    out = []
    for j in range(2):
        finish(j)
        if j == 0:
            ulp[0, head, :] = ulp[0, head, :] - mm3(edge0, cxp)
        else:
            ulp[1, tail, :] = ulp[1, tail, :] - mm3(edge1, cxp)
        out.append(pltpu.make_async_copy(lp.at[j], p_h.at[j], out_sem.at[2 * j]))
        out.append(pltpu.make_async_copy(ulp.at[j], up_h.at[j], out_sem.at[2 * j + 1]))
        out[-2].start()
        out[-1].start()
    for c in s2:
        c.wait()
    total = gath2[0]
    for q in range(1, n_grp):
        total = total + gath2[q]
    sums_out[...] = total

    @pl.when(has_next)
    def _():
        d_next.wait_send()
        b_next.wait_send()
        c_next.wait_send()

    @pl.when(has_prev)
    def _():
        d_prev.wait_send()
        b_prev.wait_send()
        c_prev.wait_send()

    @pl.when(even)
    def _():
        b_copy.wait_send()

        @pl.when(jnp.logical_not(first_plane))
        def _():
            t_even.wait_send()
            t_odd.wait_send()

    @pl.when(odd)
    def _():
        q_copy.wait_send()

        @pl.when(jnp.logical_not(last_plane))
        def _():
            y_odd.wait_send()
            y_even.wait_send()

    out_d.wait()
    for c in out:
        c.wait()


def shards(
    schur,
    local_inverse,
    coupling,
    basis,
    coarse_map,
    coarse_count,
    diag_inverse,
    chain_factor,
    residual,
    direction,
    rz_prev,
):
    n_sub, n_grp = lax.axis_size("sub"), lax.axis_size("grp")
    subs, faces, cols = residual.shape
    share = coupling.shape[1]
    slots = basis.shape[1]
    blk = diag_inverse.shape[1]
    part = cols // n_sub
    wide = n_sub * LANE
    vm = pltpu.VMEM
    dma = pltpu.SemaphoreType.DMA
    whole = pl.BlockSpec(memory_space=pltpu.VMEM)
    far = pl.BlockSpec(memory_space=pl.ANY)
    strip = vm((part, blk), F32)
    scratch = [
        vm(schur.shape, BF16),
        vm(schur.shape, BF16),
        vm(diag_inverse.shape, F32),
        vm(chain_factor.shape, F32),
        vm(residual.shape, F32),
        vm(residual.shape, F32),
        vm(residual.shape, BF16),
        vm((faces, cols), BF16),
        vm((faces, cols), BF16),
        vm(residual.shape, F32),
        vm(residual.shape, F32),
        vm(residual.shape, F32),
        vm((subs, faces, LANE), BF16),
        vm((subs, faces, 3 * LANE), BF16),
        vm((2, slots + 8, share), F32),
        vm((2, share, LANE), F32),
        vm((8, LANE), jnp.int32),
        vm((8, LANE), F32),
        vm((n_sub, 8, LANE), F32),
        vm((n_sub, part, LANE), F32),
        vm((n_sub, part, LANE), F32),
        vm((blk, blk), F32),
        vm((blk, blk), F32),
        vm((6, blk, blk), BF16),
        vm((4, blk, blk), BF16),
        vm((4, blk, wide), BF16),
        strip,
        strip,
        strip,
        strip,
        strip,
        strip,
        strip,
        strip,
        strip,
        strip,
        strip,
        strip,
        vm((n_sub, part, LANE), F32),
        vm((n_sub, part, LANE), F32),
        vm((2 * slots, cols), F32),
        vm((2, slots, cols), F32),
        vm((2, share, cols), F32),
        vm((2, share, cols), F32),
        vm((2, slots + 8, share), F32),
        vm((2 * slots, cols), F32),
        vm((8, cols), F32),
        vm((n_sub, 8, cols), F32),
        vm((8, cols), F32),
        vm((n_grp, 8, cols), F32),
        dma((7,)),
        dma((5,)),
        dma((2, n_sub)),
        dma((2, n_sub)),
        dma((2, 1)),
        dma((2, 1)),
        dma((2, 2)),
        dma((2, 1)),
        dma((2, 2)),
        dma((2, n_sub)),
        dma((2, 2)),
        dma((2, 2)),
        dma((2, 2)),
        dma((2, 2)),
        dma((2, n_sub)),
        dma((2, n_grp)),
    ]
    big = jax.ShapeDtypeStruct(residual.shape, F32)
    precond, applied_p, applied_d, dots = pl.pallas_call(
        functools.partial(kernel, n_sub, n_grp),
        out_shape=(big, big, big, jax.ShapeDtypeStruct((8, cols), F32)),
        in_specs=[pl.BlockSpec(memory_space=pltpu.SMEM)] + [whole] * 3 + [far] * 6,
        out_specs=(far, far, far, whole),
        scratch_shapes=scratch,
        compiler_params=pltpu.CompilerParams(
            collective_id=0, has_side_effects=True, vmem_limit_bytes=60 * 2**20
        ),
    )(
        coarse_count,
        coupling,
        basis,
        coarse_map,
        schur,
        local_inverse,
        diag_inverse,
        chain_factor,
        residual,
        direction,
    )
    beta = dots[0] / rz_prev
    step = dots[0] / (dots[1] + beta * (dots[2] + beta * dots[3]))
    return (
        step * (precond + beta * direction),
        residual - step * (applied_p + beta * applied_d),
    )


def solution(mesh):
    return jax.shard_map(
        shards,
        mesh=mesh,
        in_specs=(
            P(("sub", "grp"), None, None),
            P(("sub", "grp"), None, None),
            P(("sub", "grp"), None),
            P(("sub", "grp"), None, None),
            P(("sub", "grp"), None),
            P(("sub", "grp")),
            P("grp", None, None),
            P("grp", None, None),
            P(("sub", "grp"), None, None),
            P(("sub", "grp"), None, None),
            P(),
        ),
        out_specs=(P(("sub", "grp"), None, None), P(("sub", "grp"), None, None)),
        check_vma=False,
    )
```
